32 devices in a mesh: tm: 8 (over z, core), tile: 4 (over y, x).
Axes of the slice: x: 2, y: 2, z: 4, core: 2. Of those that a mesh axis runs over, the one named last changes fastest.
Arguments:
- obs_values: bfloat16 [8, 8192, 128], P('tm', 'tile'), may hold values from -6 to 6
- obs_weight: bfloat16 [8, 8192, 128], P('tm', 'tile'), may hold values from 0.19921875 to 2
- obs_count: int32 [8, 8192], P('tm', 'tile'), may hold values from 32 to 128
- dest_tile: int32 [8, 8192, 1], P('tm', 'tile'), may hold values from 0 to 3; in each aligned block of 2048 rows (0 to 2047, 2048 to 4095, ..., all dimensions but the last counted through in order) at most 1024 rows name the same one
- jac_index: int32 [8, 8192], P('tm', 'tile'), may hold values from 0 to 255
- jacobian: bfloat16 [8, 1024, 128, 128], P('tm', 'tile'), may hold values from -0.5 to 0.5
- jac_state: int32 [8, 1024], P('tm', 'tile'), may hold values from 0 to 63
- corr_blocks: bfloat16 [8, 192, 128, 128], P('tm', 'tile'), may hold values from -0.625 to 0.625
- corr_row: int32 [8, 192], P('tm', 'tile'), may hold values from 0 to 63
- corr_col: int32 [8, 192], P('tm', 'tile'), may hold values from 0 to 63
- time_coupling: bfloat16 [8, 256, 128], P('tm', 'tile'), may hold values from 0.19921875 to 0.59765625
Outputs:
- product: bfloat16 [8, 8192, 128], P('tm', 'tile')
The draws below stay inside these ranges and needn't reach their ends.
Inputs may be any that keep to these rules, and one draw needn't show every extreme that they name: `dest_tile`: in the rows of one device, no tile is named by more than 1024 observation blocks, a bound that some block reaches.
All inputs are finite; a program needn't handle non-finite values.
Results may differ from the reference program's by a relative error of at most 0.0075.
Values may be sent and summed in bfloat16 or wider, within the bound.
A program may use at most 64 MiB of HBM per device.

```python
import math
import jax
import jax.numpy as jnp
import numpy as np
from jax import lax

BLOCK = 128
OBS_DEV = 2048
JAC_DEV = 256
STATE_DEV = 64
CORR_DEV = 48
TILES = 4
WINDOWS = 8
CAP = 1024
OBS_ROW = 8192
JAC_ROW = 1024
STATE_ROW = 256
CORR_ROW = 192


def touch_ends(values, own_key, smallest, top_value):
    longest = values.shape.index(max(values.shape))
    spots = []
    for shift in (0, 1):
        where = [jax.random.randint(jax.random.fold_in(own_key, axis), (), 0, length) for axis, length in enumerate(values.shape)]
        where[longest] = (where[longest] + shift) % values.shape[longest]
        spots.append(tuple(where))
    return values.at[spots[0]].set(smallest).at[spots[1]].set(top_value)


def steps_of(stream_key, shape, pieces, least, high):
    def one(position, blocks):
        draws = jax.random.uniform(jax.random.fold_in(jax.random.fold_in(stream_key, 6), position), (blocks,), jnp.float32, least / len(pieces), high / len(pieces))
        return jnp.repeat(jnp.exp(draws), shape[position] // blocks).reshape((-1,) + (1,) * (len(shape) - position - 1))

    loudness = one(*pieces[0])
    for cut in pieces[1:]:
        loudness = loudness * one(*cut)
    return loudness


def shared_out(key, own, number, rows, amount, top, reach, skew):
    order = jax.random.permutation(key, amount)
    packed, common = shares(amount, rows * top, reach, skew, True), shares(amount, rows * top, reach, skew, False)
    places = jnp.arange(amount)

    def named(sizes, rotation):
        used = int((sizes > 0).sum())
        fixed = max(1, used // 4)
        moved = fixed + (places - fixed + rotation * (used - fixed)) % max(1, amount - fixed)
        return jnp.zeros((amount,), jnp.int32).at[order[jnp.where(places < fixed, places, moved)]].set(jnp.asarray(sizes, jnp.int32))

    sizes = jnp.where(number % 4 == 0, named(packed, number // 4), named(common, number - number // 4 - 1))
    mixed = jax.random.permutation(jax.random.fold_in(own, 3), amount)
    donor, taker = mixed[0:amount // 2 * 2:2], mixed[1:amount // 2 * 2:2]
    margin = jnp.minimum(sizes[donor] - 1, reach - sizes[taker]) // 2
    margin = jnp.where((donor == order[0]) | (taker == order[0]) | (sizes[taker] == 0), 0, jnp.maximum(margin, 0))
    moved = jax.random.randint(jax.random.fold_in(own, 4), (amount // 2,), 0, 1 << 20) % (margin + 1)
    sizes = sizes.at[donor].add(-moved).at[taker].add(moved)
    members = jnp.searchsorted(jnp.cumsum(sizes), jnp.arange(rows * top), side="right").astype(jnp.int32)
    table = members.reshape(top, rows).T
    table = table[jax.random.permutation(jax.random.fold_in(own, 1), rows)]
    rotation = jax.random.randint(jax.random.fold_in(own, 2), (rows, 1), 0, top)
    return jnp.take_along_axis(table, (jnp.arange(top)[None, :] + rotation) % top, axis=1)


def shares(count, total, limit, lean, full):
    loads = [(1 << 20) // math.isqrt(grade ** lean) + 1 for grade in range(1, count + 1)]
    largest = limit if full else min(limit, max(-(-total // count), total * loads[0] // sum(loads)))
    least = 1 if total - largest >= count - 1 else 0
    counts, spare = [largest] + [least] * (count - 1), total - largest - least * (count - 1)
    while spare > 0:
        movable = [i for i in range(1, count) if counts[i] < largest] or [i for i in range(1, count) if counts[i] < limit]
        pool, budget = sum([loads[i] for i in movable]), spare
        for i in movable:
            addition = min(limit - counts[i], max(1, budget * loads[i] // pool), spare)
            counts[i] = counts[i] + addition
            spare = spare - addition
    return np.array(counts)


def bell_draw(rng, shape, deviation, most, pieces=(), kind=jnp.bfloat16):
    entries = deviation * jax.random.normal(rng, shape, jnp.float32)
    if pieces:
        entries = entries * steps_of(rng, shape, pieces, -0.22, 0.18)
    return jnp.clip(entries, -most, most).astype(kind)


def setup_inputs(seed: int = 0) -> dict:
    splits = jax.random.split(jax.random.key(seed), 12)
    obs_values = bell_draw(splits[0], (WINDOWS, OBS_ROW, BLOCK), 1.0, 6.0, ((0, 8), (1, 4)))
    obs_weight = jnp.clip(jnp.exp(math.log(2.0) - 2.306499 * jax.random.uniform(splits[1], (WINDOWS, OBS_ROW, BLOCK), jnp.float32) ** steps_of(splits[1], (WINDOWS, OBS_ROW, BLOCK), ((0, 8), (1, 4)), -0.2, 0.2)), 0.19921875, 2.0).astype(jnp.bfloat16)
    obs_count = touch_ends(jax.random.randint(splits[2], (WINDOWS, OBS_ROW), BLOCK // 4, BLOCK + 1), jax.random.fold_in(splits[2], 1), BLOCK // 4, BLOCK).astype(jnp.int32)
    dest_tile_keys = jax.random.split(jax.random.fold_in(splits[3], 1), WINDOWS * OBS_ROW // OBS_DEV)
    dest_tile_turns = jax.random.permutation(jax.random.fold_in(splits[3], 3), WINDOWS * OBS_ROW // OBS_DEV)
    dest_tile = jax.vmap(lambda own, number: shared_out(jax.random.fold_in(splits[3], 2), own, number, OBS_DEV, TILES, 1, CAP, 2))(dest_tile_keys, dest_tile_turns).reshape((WINDOWS, OBS_ROW, 1))
    jac_index = touch_ends(jax.random.randint(splits[4], (WINDOWS, OBS_ROW), 0, JAC_DEV), jax.random.fold_in(splits[4], 1), 0, JAC_DEV - 1).astype(jnp.int32)
    jacobian = bell_draw(splits[5], (WINDOWS, JAC_ROW, BLOCK, BLOCK), BLOCK ** -0.5, 0.5, ((0, 8), (1, 4)))
    jac_state = touch_ends(jax.random.randint(splits[6], (WINDOWS, JAC_ROW), 0, STATE_DEV), jax.random.fold_in(splits[6], 1), 0, STATE_DEV - 1).astype(jnp.int32)
    corr_blocks = bell_draw(splits[7], (WINDOWS, CORR_ROW, BLOCK, BLOCK), (BLOCK * CORR_DEV // STATE_DEV) ** -0.5, 0.625, ((0, 8), (1, 4)))
    corr_row = touch_ends(jax.random.randint(splits[8], (WINDOWS, CORR_ROW), 0, STATE_DEV), jax.random.fold_in(splits[8], 1), 0, STATE_DEV - 1).astype(jnp.int32)
    corr_col = touch_ends(jax.random.randint(splits[9], (WINDOWS, CORR_ROW), 0, STATE_DEV), jax.random.fold_in(splits[9], 1), 0, STATE_DEV - 1).astype(jnp.int32)
    time_coupling = jnp.clip(0.19921875 + 0.3984375 * jax.random.uniform(splits[10], (WINDOWS, STATE_ROW, BLOCK), jnp.float32) ** steps_of(splits[10], (WINDOWS, STATE_ROW, BLOCK), ((0, 8), (1, 4)), -0.2, 0.2), 0.19921875, 0.59765625).astype(jnp.bfloat16)
    return {"obs_values": obs_values, "obs_weight": obs_weight, "obs_count": obs_count, "dest_tile": dest_tile, "jac_index": jac_index, "jacobian": jacobian, "jac_state": jac_state, "corr_blocks": corr_blocks, "corr_row": corr_row, "corr_col": corr_col, "time_coupling": time_coupling}


def reference(obs_values, obs_weight, obs_count, dest_tile, jac_index, jacobian, jac_state, corr_blocks, corr_row, corr_col, time_coupling):
    lane_index = jnp.arange(BLOCK, dtype=jnp.int32)
    keeping = (lane_index[None, None, :] < obs_count[:, :, None]).astype(jnp.float32)
    weighted = (obs_values.astype(jnp.float32) * obs_weight.astype(jnp.float32) * keeping).astype(jnp.bfloat16)
    bin_index = (dest_tile[:, :, 0] * JAC_DEV + jac_index).astype(jnp.int32)
    jac_tiles = jnp.arange(JAC_ROW, dtype=jnp.int32) // JAC_DEV
    state_index = (jac_tiles[None, :] * STATE_DEV + jac_state).astype(jnp.int32)
    corr_tiles = jnp.arange(CORR_ROW, dtype=jnp.int32) // CORR_DEV
    write_index = (corr_tiles[None, :] * STATE_DEV + corr_row).astype(jnp.int32)
    read_index = (corr_tiles[None, :] * STATE_DEV + corr_col).astype(jnp.int32)

    def spatial_part(inputs):
        weighted_t, bins_t, jac_t, state_t, corr_t, writes_t, reads_t = inputs
        summed = jax.ops.segment_sum(weighted_t.astype(jnp.float32), bins_t, num_segments=JAC_ROW)
        merged = summed.astype(jnp.bfloat16)
        spread = jnp.einsum('kij,ki->kj', jac_t.astype(jnp.float32), merged.astype(jnp.float32))
        state = jax.ops.segment_sum(spread, state_t, num_segments=STATE_ROW).astype(jnp.bfloat16)
        source = state[reads_t]
        mixing = jnp.einsum('cij,cj->ci', corr_t.astype(jnp.float32), source.astype(jnp.float32))
        return jax.ops.segment_sum(mixing, writes_t, num_segments=STATE_ROW).astype(jnp.bfloat16)

    spatial = lax.map(spatial_part, (weighted, bin_index, jacobian, state_index, corr_blocks, write_index, read_index))
    blank_state = jnp.zeros_like(spatial[:1])
    earlier = jnp.concatenate([blank_state, spatial[:-1]], axis=0)
    later_state = jnp.concatenate([spatial[1:], blank_state], axis=0)
    later_coupling = jnp.concatenate([time_coupling[1:], jnp.zeros_like(time_coupling[:1])], axis=0)
    coupled = (spatial.astype(jnp.float32) + time_coupling.astype(jnp.float32) * earlier.astype(jnp.float32)
               + later_coupling.astype(jnp.float32) * later_state.astype(jnp.float32)).astype(jnp.bfloat16)

    def forward_part(inputs):
        coupled_t, jac_t, state_t, bins_t = inputs
        local_state = coupled_t[state_t]
        model_obs = jnp.einsum('kij,kj->ki', jac_t.astype(jnp.float32), local_state.astype(jnp.float32)).astype(jnp.bfloat16)
        return model_obs[bins_t]

    picked = lax.map(forward_part, (coupled, jacobian, state_index, bin_index))
    return (picked.astype(jnp.float32) * keeping).astype(jnp.bfloat16)
```

```python
import functools

import jax
import jax.numpy as jnp
from jax import lax
from jax.experimental import pallas as pl
from jax.experimental.pallas import tpu as pltpu
from jax.sharding import PartitionSpec as P

MESH = pl.DeviceIdType.MESH
GROUP = 16
CHUNKS = 4


def kernel(
    tiles,
    windows,
    count_ref,
    target_ref,
    column_ref,
    values_ref,
    weight_ref,
    jac_hbm,
    jac_state,
    corr_hbm,
    corr_row,
    corr_col,
    coupling_ref,
    out_ref,
    jac,
    corr,
    picker,
    weighted,
    keeping,
    partial,
    arrived,
    portion,
    merged,
    state,
    coupled,
    local,
    source,
    spatial_send,
    spatial_recv,
    coupling_recv,
    jac_sem,
    corr_sem,
    sum_send,
    sum_recv,
    time_send,
    time_recv,
    image_send,
    image_recv,
):
    f32, bf16 = jnp.float32, jnp.bfloat16
    me = lax.axis_index("tile")
    now = lax.axis_index("tm")
    width = values_ref.shape[1]
    obs_rows = count_ref.shape[0]
    jac_total = merged.shape[0]
    state_total = state.shape[0]
    corr_total = corr_row.shape[1]
    has_earlier, has_later = now > 0, now < windows - 1
    peers = [lax.rem(me + step, tiles) for step in range(tiles)]

    barrier = pltpu.get_barrier_semaphore()
    for peer in peers[1:]:
        pl.semaphore_signal(barrier, inc=1, device_id={"tile": peer}, device_id_type=MESH)

    @pl.when(has_earlier)
    def _():
        pl.semaphore_signal(barrier, inc=1, device_id={"tm": now - 1}, device_id_type=MESH)

    @pl.when(has_later)
    def _():
        pl.semaphore_signal(barrier, inc=1, device_id={"tm": now + 1}, device_id_type=MESH)

    jac_part = jac.shape[0] // CHUNKS
    jac_copies = []
    for part in range(CHUNKS):
        rows = pl.ds(part * jac_part, jac_part)
        jac_copies.append(pltpu.make_async_copy(jac_hbm.at[rows], jac.at[rows], jac_sem.at[part]))
        jac_copies[-1].start()
    corr_copy = pltpu.make_async_copy(corr_hbm, corr, corr_sem)
    corr_copy.start()

    lane = lax.broadcasted_iota(jnp.int32, (width, width), 1)
    eye = lax.broadcasted_iota(jnp.int32, (width, width), 0) == lane
    ones = jnp.ones((width, width), bf16)

    def upright(ref, row):
        spread = jnp.where(eye, ref[pl.ds(row, 1), :].astype(f32), 0.0).astype(bf16)
        return jnp.dot(spread, ones, preferred_element_type=f32)

    def weigh(row, carry):
        rows = pl.ds(pl.multiple_of(row * width, width), width)
        keep = (lane.astype(f32) < upright(count_ref, row)).astype(f32)
        keeping[rows, :] = keep.astype(bf16)
        weighted[rows, :] = (
            values_ref[rows, :].astype(f32) * weight_ref[rows, :].astype(f32) * keep
        ).astype(bf16)
        return carry

    lax.fori_loop(0, obs_rows, weigh, 0, unroll=4)

    bins = lax.broadcasted_iota(jnp.int32, (jac_total, width), 0)

    def partial_sum(tile):
        def add(row, total):
            wanted = jnp.where(
                target_ref[pl.ds(row, 1), :] == tile, column_ref[pl.ds(row, 1), :], -1
            )
            pick = jnp.where(bins == wanted, 1.0, 0.0).astype(bf16)
            rows = pl.ds(pl.multiple_of(row * width, width), width)
            return total + jnp.dot(pick, weighted[rows, :], preferred_element_type=f32)

        return lax.fori_loop(0, obs_rows, add, jnp.zeros((jac_total, width), f32), unroll=4)

    pl.semaphore_wait(
        barrier,
        tiles - 1 + jnp.where(has_earlier, 1, 0) + jnp.where(has_later, 1, 0),
    )

    def coupling_copy():
        return pltpu.make_async_remote_copy(
            src_ref=coupling_ref,
            dst_ref=coupling_recv,
            send_sem=time_send.at[2],
            recv_sem=time_recv.at[2],
            device_id={"tm": now - 1},
            device_id_type=MESH,
        )

    def spatial_copy(slot, to):
        return pltpu.make_async_remote_copy(
            src_ref=spatial_send,
            dst_ref=spatial_recv.at[slot],
            send_sem=time_send.at[slot],
            recv_sem=time_recv.at[slot],
            device_id={"tm": to},
            device_id_type=MESH,
        )

    @pl.when(has_earlier)
    def _():
        coupling_copy().start()

    sum_copies = []
    for step in range(1, tiles):
        partial[step - 1] = partial_sum(peers[step]).astype(bf16)
        copy = pltpu.make_async_remote_copy(
            src_ref=partial.at[step - 1],
            dst_ref=arrived.at[step - 1],
            send_sem=sum_send.at[step - 1],
            recv_sem=sum_recv.at[step - 1],
            device_id={"tile": peers[step]},
            device_id_type=MESH,
        )
        copy.start()
        sum_copies.append(copy)
    merged[...] = partial_sum(me)

    lane_f = lane.astype(f32)

    def pick_rows(row, carry):
        rows = pl.ds(pl.multiple_of(row * width, width), width)
        column = upright(column_ref, row)
        target = upright(target_ref, row)
        for tile in range(tiles):
            wanted = jnp.where(target == float(tile), column, -1.0)
            for part in range(jac_total // width):
                start = tile * jac_total + part * width
                picker[rows, start : start + width] = jnp.where(
                    wanted == lane_f + float(part * width), 1.0, 0.0
                ).astype(bf16)
        return carry

    lax.fori_loop(0, obs_rows, pick_rows, 0)

    for step in range(1, tiles):
        sum_copies[step - 1].wait_recv()
        merged[...] += arrived[step - 1].astype(f32)
    merged[...] = merged[...].astype(bf16).astype(f32)
    for copy in jac_copies:
        copy.wait()

    state_ids = lax.broadcasted_iota(jnp.int32, (state_total, width), 0)

    def to_state(group, total):
        pieces = []
        for k in range(GROUP):
            block = group * GROUP + k
            pieces.append(
                jnp.where(
                    state_ids == jac_state[0, block], merged[pl.ds(block, 1), :], 0.0
                ).astype(bf16)
            )
        rows = pl.ds(pl.multiple_of(group * GROUP * width, GROUP * width), GROUP * width)
        return total + jnp.dot(
            jnp.concatenate(pieces, axis=1), jac[rows, :], preferred_element_type=f32
        )

    blank = jnp.zeros((state_total, width), f32)
    state[...] = (
        lax.fori_loop(0, jac_total // GROUP, to_state, blank).astype(bf16).astype(f32)
    )
    corr_copy.wait()

    def correlate(group, total):
        for k in range(8):
            block = group * 8 + k
            piece = jnp.where(
                state_ids == corr_row[0, block], state[pl.ds(corr_col[0, block], 1), :], 0.0
            ).astype(bf16)
            rows = pl.ds(pl.multiple_of(block * width, width), width)
            total = total + lax.dot_general(
                piece, corr[rows, :], (((1,), (1,)), ((), ())), preferred_element_type=f32
            )
        return total

    spatial = lax.fori_loop(0, corr_total // 8, correlate, blank).astype(bf16)
    spatial_send[...] = spatial

    @pl.when(has_later)
    def _():
        spatial_copy(0, now + 1).start()

    @pl.when(has_earlier)
    def _():
        spatial_copy(1, now - 1).start()

    @pl.when(has_earlier)
    def _():
        spatial_copy(0, now - 1).wait_recv()

    @pl.when(now == 0)
    def _():
        spatial_recv[0] = jnp.zeros((state_total, width), bf16)

    @pl.when(has_later)
    def _():
        coupling_copy().wait_recv()
        spatial_copy(1, now + 1).wait_recv()

    @pl.when(now == windows - 1)
    def _():
        spatial_recv[1] = jnp.zeros((state_total, width), bf16)
        coupling_recv[...] = jnp.zeros((state_total, width), bf16)

    coupled[...] = (
        (
            spatial.astype(f32)
            + coupling_ref[...].astype(f32) * spatial_recv[0].astype(f32)
            + coupling_recv[...].astype(f32) * spatial_recv[1].astype(f32)
        )
        .astype(bf16)
        .astype(f32)
    )

    def fetch(group, carry):
        for k in range(GROUP):
            block = group * GROUP + k
            local[pl.ds(block, 1), :] = coupled[pl.ds(jac_state[0, block], 1), :]
        return carry

    lax.fori_loop(0, jac_total // GROUP, fetch, 0)

    group_ids = lax.broadcasted_iota(jnp.int32, (GROUP, width), 0)

    def images(group, carry):
        first = pl.multiple_of(group * GROUP, GROUP)
        rows = pl.ds(pl.multiple_of(group * GROUP * width, GROUP * width), GROUP * width)
        every = lax.dot_general(
            local[pl.ds(first, GROUP), :].astype(bf16),
            jac[rows, :],
            (((1,), (1,)), ((), ())),
            preferred_element_type=f32,
        )
        own = every[:, :width]
        for k in range(1, GROUP):
            own = jnp.where(group_ids == k, every[:, k * width : (k + 1) * width], own)
        portion[pl.ds(pl.multiple_of(me * jac_total + group * GROUP, GROUP), GROUP), :] = (
            own.astype(bf16)
        )
        return carry

    image_part = jac_total // CHUNKS
    groups = image_part // GROUP

    def image_copy(part, step):
        rows = pl.ds(pl.multiple_of(me * jac_total + part * image_part, image_part), image_part)
        return pltpu.make_async_remote_copy(
            src_ref=portion.at[rows],
            dst_ref=portion.at[rows],
            send_sem=image_send.at[part, step - 1],
            recv_sem=image_recv.at[part, step - 1],
            device_id={"tile": peers[step]},
            device_id_type=MESH,
        )

    for part in range(CHUNKS):
        lax.fori_loop(part * groups, (part + 1) * groups, images, 0)
        for step in range(1, tiles):
            image_copy(part, step).start()
    for part in range(CHUNKS):
        for step in range(1, tiles):
            image_copy(part, step).wait_recv()

    out_rows = 2 * width

    def gather(row, carry):
        rows = pl.ds(pl.multiple_of(row * out_rows, out_rows), out_rows)
        gathered = jnp.dot(picker[rows, :], portion[...], preferred_element_type=f32)
        out_ref[rows, :] = (gathered * keeping[rows, :].astype(f32)).astype(bf16)
        return carry

    lax.fori_loop(0, obs_rows // 2, gather, 0)

    for copy in sum_copies:
        copy.wait_send()
    for part in range(CHUNKS):
        for step in range(1, tiles):
            image_copy(part, step).wait_send()

    @pl.when(has_later)
    def _():
        spatial_copy(0, now + 1).wait_send()

    @pl.when(has_earlier)
    def _():
        spatial_copy(1, now - 1).wait_send()
        coupling_copy().wait_send()


def shards(
    tiles,
    windows,
    obs_values,
    obs_weight,
    obs_count,
    dest_tile,
    jac_index,
    jacobian,
    jac_state,
    corr_blocks,
    corr_row,
    corr_col,
    time_coupling,
):
    f32, bf16 = jnp.float32, jnp.bfloat16
    _, obs_total, width = obs_values.shape
    jac_total = jacobian.shape[1]
    corr_total = corr_blocks.shape[1]
    state_total = time_coupling.shape[1]
    vmem = pl.BlockSpec(memory_space=pltpu.VMEM)
    smem = pl.BlockSpec(memory_space=pltpu.SMEM)
    hbm = pl.BlockSpec(memory_space=pl.ANY)
    dma = pltpu.SemaphoreType.DMA
    out = pl.pallas_call(
        functools.partial(kernel, tiles, windows),
        out_shape=jax.ShapeDtypeStruct((obs_total, width), bf16),
        in_specs=[vmem] * 5 + [hbm, smem, hbm, smem, smem, vmem],
        out_specs=vmem,
        scratch_shapes=[
            pltpu.VMEM((jac_total * width, width), bf16),
            pltpu.VMEM((corr_total * width, width), bf16),
            pltpu.VMEM((obs_total, tiles * jac_total), bf16),
            pltpu.VMEM((obs_total, width), bf16),
            pltpu.VMEM((obs_total, width), bf16),
            pltpu.VMEM((tiles - 1, jac_total, width), bf16),
            pltpu.VMEM((tiles - 1, jac_total, width), bf16),
            pltpu.VMEM((tiles * jac_total, width), bf16),
            pltpu.VMEM((jac_total, width), f32),
            pltpu.VMEM((state_total, width), f32),
            pltpu.VMEM((state_total, width), f32),
            pltpu.VMEM((jac_total, width), f32),
            pltpu.VMEM((corr_total, width), f32),
            pltpu.VMEM((state_total, width), bf16),
            pltpu.VMEM((2, state_total, width), bf16),
            pltpu.VMEM((state_total, width), bf16),
            dma((CHUNKS,)),
            dma,
            dma((tiles - 1,)),
            dma((tiles - 1,)),
            dma((3,)),
            dma((3,)),
            dma((CHUNKS, tiles - 1)),
            dma((CHUNKS, tiles - 1)),
        ],
        compiler_params=pltpu.CompilerParams(
            collective_id=0, has_side_effects=True, vmem_limit_bytes=56 * 1024 * 1024
        ),
        name="dual_space",
    )(
        obs_count.reshape(obs_total // width, width),
        dest_tile.reshape(obs_total // width, width),
        jac_index.reshape(obs_total // width, width),
        obs_values[0],
        obs_weight[0],
        jacobian.reshape(jac_total * width, width),
        jac_state,
        corr_blocks.reshape(corr_total * width, width),
        corr_row,
        corr_col,
        time_coupling[0],
    )
    return out[None]


def solution(mesh):
    in_specs = (
        P("tm", "tile", None),
        P("tm", "tile", None),
        P("tm", "tile"),
        P("tm", "tile", None),
        P("tm", "tile"),
        P("tm", "tile", None, None),
        P("tm", "tile"),
        P("tm", "tile", None, None),
        P("tm", "tile"),
        P("tm", "tile"),
        P("tm", "tile", None),
    )
    out_specs = P("tm", "tile", None)
    body = functools.partial(shards, mesh.shape["tile"], mesh.shape["tm"])
    return jax.shard_map(body, mesh=mesh, in_specs=in_specs, out_specs=out_specs, check_vma=False)
```

```python
import functools

import jax
import jax.numpy as jnp
from jax import lax
from jax.experimental import pallas as pl
from jax.experimental.pallas import tpu as pltpu
from jax.sharding import PartitionSpec as P

MESH = pl.DeviceIdType.MESH
GROUP = 16
CHUNKS = 4


def kernel(
    tiles,
    windows,
    count_ref,
    target_ref,
    column_ref,
    values_hbm,
    weight_hbm,
    jac_hbm,
    jac_state,
    corr_hbm,
    corr_row,
    corr_col,
    coupling_ref,
    out_hbm,
    values_ref,
    weight_ref,
    picks,
    out_ref,
    jac,
    corr,
    picker,
    weighted,
    keeping,
    partial,
    arrived,
    portion,
    merged,
    state,
    coupled,
    local,
    source,
    spatial_send,
    spatial_recv,
    coupling_recv,
    obs_sem,
    out_sem,
    jac_sem,
    corr_sem,
    sum_send,
    sum_recv,
    time_send,
    time_recv,
    image_send,
    image_recv,
):
    f32, bf16 = jnp.float32, jnp.bfloat16
    me = lax.axis_index("tile")
    now = lax.axis_index("tm")
    width = values_ref.shape[1]
    obs_rows = count_ref.shape[0]
    jac_total = merged.shape[0]
    state_total = state.shape[0]
    corr_total = corr_row.shape[1]
    has_earlier, has_later = now > 0, now < windows - 1
    peers = [lax.rem(me + step, tiles) for step in range(tiles)]

    obs_copies = [
        pltpu.make_async_copy(values_hbm, values_ref, obs_sem.at[0]),
        pltpu.make_async_copy(weight_hbm, weight_ref, obs_sem.at[1]),
    ]
    for copy in obs_copies:
        copy.start()
    barrier = pltpu.get_barrier_semaphore()
    for peer in peers[1:]:
        pl.semaphore_signal(barrier, inc=1, device_id={"tile": peer}, device_id_type=MESH)

    @pl.when(has_earlier)
    def _():
        pl.semaphore_signal(barrier, inc=1, device_id={"tm": now - 1}, device_id_type=MESH)

    @pl.when(has_later)
    def _():
        pl.semaphore_signal(barrier, inc=1, device_id={"tm": now + 1}, device_id_type=MESH)

    jac_part = jac.shape[0] // CHUNKS
    jac_copies = []
    for part in range(CHUNKS):
        rows = pl.ds(part * jac_part, jac_part)
        jac_copies.append(pltpu.make_async_copy(jac_hbm.at[rows], jac.at[rows], jac_sem.at[part]))
        jac_copies[-1].start()
    corr_copy = pltpu.make_async_copy(corr_hbm, corr, corr_sem)
    corr_copy.start()

    lane = lax.broadcasted_iota(jnp.int32, (width, width), 1)
    eye = lax.broadcasted_iota(jnp.int32, (width, width), 0) == lane
    ones = jnp.ones((width, width), bf16)

    def upright(ref, row):
        spread = jnp.where(eye, ref[pl.ds(row, 1), :].astype(f32), 0.0).astype(bf16)
        return jnp.dot(spread, ones, preferred_element_type=f32)

    def weigh(row, carry):
        rows = pl.ds(pl.multiple_of(row * width, width), width)
        keep = (lane.astype(f32) < upright(count_ref, row)).astype(f32)
        keeping[rows, :] = keep.astype(bf16)
        weighted[rows, :] = (
            values_ref[rows, :].astype(f32) * weight_ref[rows, :].astype(f32) * keep
        ).astype(bf16)
        return carry


    bins = lax.broadcasted_iota(jnp.int32, (jac_total, width), 0)

    def pick_tile(tile, slot):
        def one(row, carry):
            wanted = jnp.where(
                target_ref[pl.ds(row, 1), :] == tile, column_ref[pl.ds(row, 1), :], -1
            )
            columns = pl.ds(pl.multiple_of(row * width, width), width)
            picks[slot, :, columns] = jnp.where(bins == wanted, 1.0, 0.0).astype(bf16)
            return carry

        lax.fori_loop(0, obs_rows, one, 0, unroll=True)

    def partial_sum(slot):
        return jnp.dot(picks[slot], weighted[...], preferred_element_type=f32)

    turns = [*range(1, tiles), 0]
    pick_tile(peers[turns[0]], 0)
    for copy in obs_copies:
        copy.wait()
    lax.fori_loop(0, obs_rows, weigh, 0, unroll=True)

    pl.semaphore_wait(
        barrier,
        tiles - 1 + jnp.where(has_earlier, 1, 0) + jnp.where(has_later, 1, 0),
    )

    def coupling_copy():
        return pltpu.make_async_remote_copy(
            src_ref=coupling_ref,
            dst_ref=coupling_recv,
            send_sem=time_send.at[2],
            recv_sem=time_recv.at[2],
            device_id={"tm": now - 1},
            device_id_type=MESH,
        )

    def spatial_copy(slot, to):
        return pltpu.make_async_remote_copy(
            src_ref=spatial_send,
            dst_ref=spatial_recv.at[slot],
            send_sem=time_send.at[slot],
            recv_sem=time_recv.at[slot],
            device_id={"tm": to},
            device_id_type=MESH,
        )

    @pl.when(has_earlier)
    def _():
        coupling_copy().start()

    sum_copies = []
    for turn, step in enumerate(turns):
        if turn > 0:
            pick_tile(peers[step], turn % 2)
        if step == 0:
            merged[...] = partial_sum(turn % 2)
            continue
        partial[step - 1] = partial_sum(turn % 2).astype(bf16)
        copy = pltpu.make_async_remote_copy(
            src_ref=partial.at[step - 1],
            dst_ref=arrived.at[step - 1],
            send_sem=sum_send.at[step - 1],
            recv_sem=sum_recv.at[step - 1],
            device_id={"tile": peers[step]},
            device_id_type=MESH,
        )
        copy.start()
        sum_copies.append(copy)

    lane_f = lane.astype(f32)

    def pick_rows(row, carry):
        rows = pl.ds(pl.multiple_of(row * width, width), width)
        column = upright(column_ref, row)
        target = upright(target_ref, row)
        for tile in range(tiles):
            wanted = jnp.where(target == float(tile), column, -1.0)
            for part in range(jac_total // width):
                start = tile * jac_total + part * width
                picker[rows, start : start + width] = jnp.where(
                    wanted == lane_f + float(part * width), 1.0, 0.0
                ).astype(bf16)
        return carry

    lax.fori_loop(0, obs_rows, pick_rows, 0, unroll=2)

    for step in range(1, tiles):
        sum_copies[step - 1].wait_recv()
        merged[...] += arrived[step - 1].astype(f32)
    merged[...] = merged[...].astype(bf16).astype(f32)
    for copy in jac_copies:
        copy.wait()

    state_ids = lax.broadcasted_iota(jnp.int32, (state_total, width), 0)

    def to_state(group, total):
        pieces = []
        for k in range(GROUP):
            block = group * GROUP + k
            pieces.append(
                jnp.where(
                    state_ids == jac_state[0, block], merged[pl.ds(block, 1), :], 0.0
                ).astype(bf16)
            )
        rows = pl.ds(pl.multiple_of(group * GROUP * width, GROUP * width), GROUP * width)
        return total + jnp.dot(
            jnp.concatenate(pieces, axis=1), jac[rows, :], preferred_element_type=f32
        )

    blank = jnp.zeros((state_total, width), f32)
    state[...] = (
        lax.fori_loop(0, jac_total // GROUP, to_state, blank, unroll=4).astype(bf16).astype(f32)
    )
    corr_copy.wait()

    def correlate(group, total):
        for k in range(8):
            block = group * 8 + k
            piece = jnp.where(
                state_ids == corr_row[0, block], state[pl.ds(corr_col[0, block], 1), :], 0.0
            ).astype(bf16)
            rows = pl.ds(pl.multiple_of(block * width, width), width)
            total = total + lax.dot_general(
                piece, corr[rows, :], (((1,), (1,)), ((), ())), preferred_element_type=f32
            )
        return total

    spatial = lax.fori_loop(0, corr_total // 8, correlate, blank, unroll=True).astype(bf16)
    spatial_send[...] = spatial

    @pl.when(has_later)
    def _():
        spatial_copy(0, now + 1).start()

    @pl.when(has_earlier)
    def _():
        spatial_copy(1, now - 1).start()

    @pl.when(has_earlier)
    def _():
        spatial_copy(0, now - 1).wait_recv()

    @pl.when(now == 0)
    def _():
        spatial_recv[0] = jnp.zeros((state_total, width), bf16)

    @pl.when(has_later)
    def _():
        coupling_copy().wait_recv()
        spatial_copy(1, now + 1).wait_recv()

    @pl.when(now == windows - 1)
    def _():
        spatial_recv[1] = jnp.zeros((state_total, width), bf16)
        coupling_recv[...] = jnp.zeros((state_total, width), bf16)

    coupled[...] = (
        (
            spatial.astype(f32)
            + coupling_ref[...].astype(f32) * spatial_recv[0].astype(f32)
            + coupling_recv[...].astype(f32) * spatial_recv[1].astype(f32)
        )
        .astype(bf16)
        .astype(f32)
    )

    def fetch(group, carry):
        for k in range(GROUP):
            block = group * GROUP + k
            local[pl.ds(block, 1), :] = coupled[pl.ds(jac_state[0, block], 1), :]
        return carry

    lax.fori_loop(0, jac_total // GROUP, fetch, 0, unroll=True)

    group_ids = lax.broadcasted_iota(jnp.int32, (GROUP, width), 0)

    def images(group, carry):
        first = pl.multiple_of(group * GROUP, GROUP)
        rows = pl.ds(pl.multiple_of(group * GROUP * width, GROUP * width), GROUP * width)
        every = lax.dot_general(
            local[pl.ds(first, GROUP), :].astype(bf16),
            jac[rows, :],
            (((1,), (1,)), ((), ())),
            preferred_element_type=f32,
        )
        own = every[:, :width]
        for k in range(1, GROUP):
            own = jnp.where(group_ids == k, every[:, k * width : (k + 1) * width], own)
        portion[pl.ds(pl.multiple_of(me * jac_total + group * GROUP, GROUP), GROUP), :] = (
            own.astype(bf16)
        )
        return carry

    image_part = jac_total // CHUNKS
    groups = image_part // GROUP

    def image_copy(part, step):
        rows = pl.ds(pl.multiple_of(me * jac_total + part * image_part, image_part), image_part)
        return pltpu.make_async_remote_copy(
            src_ref=portion.at[rows],
            dst_ref=portion.at[rows],
            send_sem=image_send.at[part, step - 1],
            recv_sem=image_recv.at[part, step - 1],
            device_id={"tile": peers[step]},
            device_id_type=MESH,
        )

    for part in range(CHUNKS):
        lax.fori_loop(part * groups, (part + 1) * groups, images, 0, unroll=True)
        for step in range(1, tiles):
            image_copy(part, step).start()
    for part in range(CHUNKS):
        for step in range(1, tiles):
            image_copy(part, step).wait_recv()

    out_rows = obs_rows * width // CHUNKS
    out_copies = []
    for part in range(CHUNKS):
        rows = pl.ds(part * out_rows, out_rows)
        gathered = jnp.dot(picker[rows, :], portion[...], preferred_element_type=f32)
        out_ref[rows, :] = (gathered * keeping[rows, :].astype(f32)).astype(bf16)
        copy = pltpu.make_async_copy(out_ref.at[rows], out_hbm.at[rows], out_sem.at[part])
        copy.start()
        out_copies.append(copy)
    for copy in out_copies:
        copy.wait()

    for copy in sum_copies:
        copy.wait_send()
    for part in range(CHUNKS):
        for step in range(1, tiles):
            image_copy(part, step).wait_send()

    @pl.when(has_later)
    def _():
        spatial_copy(0, now + 1).wait_send()

    @pl.when(has_earlier)
    def _():
        spatial_copy(1, now - 1).wait_send()
        coupling_copy().wait_send()


def hand_over(held, out, sem):
    part = held.shape[0] // CHUNKS
    copies = []
    for k in range(CHUNKS):
        rows = pl.ds(k * part, part)
        copies.append(pltpu.make_async_copy(held.at[rows], out.at[rows], sem.at[k]))
        copies[-1].start()
    for copy in copies:
        copy.wait()


def shards(
    tiles,
    windows,
    obs_values,
    obs_weight,
    obs_count,
    dest_tile,
    jac_index,
    jacobian,
    jac_state,
    corr_blocks,
    corr_row,
    corr_col,
    time_coupling,
):
    f32, bf16 = jnp.float32, jnp.bfloat16
    _, obs_total, width = obs_values.shape
    jac_total = jacobian.shape[1]
    corr_total = corr_blocks.shape[1]
    state_total = time_coupling.shape[1]
    vmem = pl.BlockSpec(memory_space=pltpu.VMEM)
    smem = pl.BlockSpec(memory_space=pltpu.SMEM)
    hbm = pl.BlockSpec(memory_space=pl.ANY)
    dma = pltpu.SemaphoreType.DMA
    out = pl.pallas_call(
        functools.partial(kernel, tiles, windows),
        out_shape=jax.ShapeDtypeStruct((obs_total, width), bf16),
        in_specs=[vmem] * 3 + [hbm] * 3 + [smem, hbm, smem, smem, vmem],
        out_specs=hbm,
        scratch_shapes=[
            pltpu.VMEM((obs_total, width), bf16),
            pltpu.VMEM((obs_total, width), bf16),
            pltpu.VMEM((2, jac_total, obs_total), bf16),
            pltpu.VMEM((obs_total, width), bf16),
            pltpu.VMEM((jac_total * width, width), bf16),
            pltpu.VMEM((corr_total * width, width), bf16),
            pltpu.VMEM((obs_total, tiles * jac_total), bf16),
            pltpu.VMEM((obs_total, width), bf16),
            pltpu.VMEM((obs_total, width), bf16),
            pltpu.VMEM((tiles - 1, jac_total, width), bf16),
            pltpu.VMEM((tiles - 1, jac_total, width), bf16),
            pltpu.VMEM((tiles * jac_total, width), bf16),
            pltpu.VMEM((jac_total, width), f32),
            pltpu.VMEM((state_total, width), f32),
            pltpu.VMEM((state_total, width), f32),
            pltpu.VMEM((jac_total, width), f32),
            pltpu.VMEM((corr_total, width), f32),
            pltpu.VMEM((state_total, width), bf16),
            pltpu.VMEM((2, state_total, width), bf16),
            pltpu.VMEM((state_total, width), bf16),
            dma((2,)),
            dma((CHUNKS,)),
            dma((CHUNKS,)),
            dma,
            dma((tiles - 1,)),
            dma((tiles - 1,)),
            dma((3,)),
            dma((3,)),
            dma((CHUNKS, tiles - 1)),
            dma((CHUNKS, tiles - 1)),
        ],
        compiler_params=pltpu.CompilerParams(
            collective_id=0, has_side_effects=True, vmem_limit_bytes=56 * 1024 * 1024
        ),
        name="dual_space",
    )(
        obs_count.reshape(obs_total // width, width),
        dest_tile.reshape(obs_total // width, width),
        jac_index.reshape(obs_total // width, width),
        obs_values[0],
        obs_weight[0],
        jacobian.reshape(jac_total * width, width),
        jac_state,
        corr_blocks.reshape(corr_total * width, width),
        corr_row,
        corr_col,
        time_coupling[0],
    )
    out = pl.pallas_call(
        hand_over,
        out_shape=jax.ShapeDtypeStruct((obs_total, width), bf16),
        in_specs=[hbm],
        out_specs=hbm,
        scratch_shapes=[dma((CHUNKS,))],
        name="hand_over",
    )(out)
    return out[None]


def solution(mesh):
    in_specs = (
        P("tm", "tile", None),
        P("tm", "tile", None),
        P("tm", "tile"),
        P("tm", "tile", None),
        P("tm", "tile"),
        P("tm", "tile", None, None),
        P("tm", "tile"),
        P("tm", "tile", None, None),
        P("tm", "tile"),
        P("tm", "tile"),
        P("tm", "tile", None),
    )
    out_specs = P("tm", "tile", None)
    body = functools.partial(shards, mesh.shape["tile"], mesh.shape["tm"])
    return jax.shard_map(body, mesh=mesh, in_specs=in_specs, out_specs=out_specs, check_vma=False)
```

```python
import functools

import jax
import jax.numpy as jnp
from jax import lax
from jax.experimental import pallas as pl
from jax.experimental.pallas import tpu as pltpu
from jax.sharding import PartitionSpec as P

MESH = pl.DeviceIdType.MESH
GROUP = 16
CHUNKS = 4


def kernel(
    tiles,
    windows,
    count_ref,
    target_ref,
    column_ref,
    values_hbm,
    weight_hbm,
    jac_hbm,
    jac_state,
    corr_hbm,
    corr_row,
    corr_col,
    coupling_ref,
    out_hbm,
    values_ref,
    weight_ref,
    picks,
    out_ref,
    jac,
    corr,
    picker,
    weighted,
    keeping,
    partial,
    arrived,
    portion,
    merged,
    state,
    coupled,
    local,
    source,
    spatial_send,
    spatial_recv,
    coupling_recv,
    obs_sem,
    out_sem,
    jac_sem,
    corr_sem,
    sum_send,
    sum_recv,
    time_send,
    time_recv,
    image_send,
    image_recv,
):
    f32, bf16 = jnp.float32, jnp.bfloat16
    me = lax.axis_index("tile")
    now = lax.axis_index("tm")
    width = values_ref.shape[1]
    obs_rows = count_ref.shape[0]
    jac_total = merged.shape[0]
    state_total = state.shape[0]
    corr_total = corr_row.shape[1]
    has_earlier, has_later = now > 0, now < windows - 1
    peers = [lax.rem(me + step, tiles) for step in range(tiles)]

    obs_copies = [
        pltpu.make_async_copy(values_hbm, values_ref, obs_sem.at[0]),
        pltpu.make_async_copy(weight_hbm, weight_ref, obs_sem.at[1]),
    ]
    for copy in obs_copies:
        copy.start()
    barrier = pltpu.get_barrier_semaphore()
    for peer in peers[1:]:
        pl.semaphore_signal(barrier, inc=1, device_id={"tile": peer}, device_id_type=MESH)

    @pl.when(has_earlier)
    def _():
        pl.semaphore_signal(barrier, inc=1, device_id={"tm": now - 1}, device_id_type=MESH)

    @pl.when(has_later)
    def _():
        pl.semaphore_signal(barrier, inc=1, device_id={"tm": now + 1}, device_id_type=MESH)

    jac_part = jac.shape[0] // CHUNKS
    jac_copies = []
    for part in range(CHUNKS):
        rows = pl.ds(part * jac_part, jac_part)
        jac_copies.append(pltpu.make_async_copy(jac_hbm.at[rows], jac.at[rows], jac_sem.at[part]))
        jac_copies[-1].start()
    corr_copy = pltpu.make_async_copy(corr_hbm, corr, corr_sem)
    corr_copy.start()

    lane = lax.broadcasted_iota(jnp.int32, (width, width), 1)
    eye = lax.broadcasted_iota(jnp.int32, (width, width), 0) == lane
    ones = jnp.ones((width, width), bf16)

    def upright(ref, row):
        spread = jnp.where(eye, ref[pl.ds(row, 1), :].astype(f32), 0.0).astype(bf16)
        return jnp.dot(spread, ones, preferred_element_type=f32)

    def weigh(row, carry):
        rows = pl.ds(pl.multiple_of(row * width, width), width)
        keep = (lane.astype(f32) < upright(count_ref, row)).astype(f32)
        keeping[rows, :] = keep.astype(bf16)
        weighted[rows, :] = (
            values_ref[rows, :].astype(f32) * weight_ref[rows, :].astype(f32) * keep
        ).astype(bf16)
        return carry


    bins = lax.broadcasted_iota(jnp.int32, (jac_total, width), 0)

    def pick_tile(tile, slot):
        def one(row, carry):
            wanted = jnp.where(
                target_ref[pl.ds(row, 1), :] == tile, column_ref[pl.ds(row, 1), :], -1
            )
            columns = pl.ds(pl.multiple_of(row * width, width), width)
            picks[slot, :, columns] = jnp.where(bins == wanted, 1.0, 0.0).astype(bf16)
            return carry

        lax.fori_loop(0, obs_rows, one, 0, unroll=True)

    def partial_sum(slot):
        return jnp.dot(picks[slot], weighted[...], preferred_element_type=f32)

    turns = sorted(range(1, tiles), key=lambda step: -abs(step - tiles // 2)) + [0]
    pick_tile(peers[turns[0]], 0)
    for copy in obs_copies:
        copy.wait()
    lax.fori_loop(0, obs_rows, weigh, 0, unroll=True)

    pl.semaphore_wait(
        barrier,
        tiles - 1 + jnp.where(has_earlier, 1, 0) + jnp.where(has_later, 1, 0),
    )

    def coupling_copy():
        return pltpu.make_async_remote_copy(
            src_ref=coupling_ref,
            dst_ref=coupling_recv,
            send_sem=time_send.at[2],
            recv_sem=time_recv.at[2],
            device_id={"tm": now - 1},
            device_id_type=MESH,
        )

    def spatial_copy(slot, to):
        return pltpu.make_async_remote_copy(
            src_ref=spatial_send,
            dst_ref=spatial_recv.at[slot],
            send_sem=time_send.at[slot],
            recv_sem=time_recv.at[slot],
            device_id={"tm": to},
            device_id_type=MESH,
        )

    @pl.when(has_earlier)
    def _():
        coupling_copy().start()

    sum_copies = []
    for turn, step in enumerate(turns):
        if turn > 0:
            pick_tile(peers[step], turn % 2)
        if step == 0:
            merged[...] = partial_sum(turn % 2)
            continue
        partial[step - 1] = partial_sum(turn % 2).astype(bf16)
        copy = pltpu.make_async_remote_copy(
            src_ref=partial.at[step - 1],
            dst_ref=arrived.at[step - 1],
            send_sem=sum_send.at[step - 1],
            recv_sem=sum_recv.at[step - 1],
            device_id={"tile": peers[step]},
            device_id_type=MESH,
        )
        copy.start()
        sum_copies.append((step, copy))

    lane_f = lane.astype(f32)

    def pick_rows(row, carry):
        rows = pl.ds(pl.multiple_of(row * width, width), width)
        column = upright(column_ref, row)
        target = upright(target_ref, row)
        for tile in range(tiles):
            wanted = jnp.where(target == float(tile), column, -1.0)
            for part in range(jac_total // width):
                start = tile * jac_total + part * width
                picker[rows, start : start + width] = jnp.where(
                    wanted == lane_f + float(part * width), 1.0, 0.0
                ).astype(bf16)
        return carry

    lax.fori_loop(0, obs_rows // 2, pick_rows, 0, unroll=2)

    for step, copy in sum_copies:
        copy.wait_recv()
        merged[...] += arrived[step - 1].astype(f32)
    merged[...] = merged[...].astype(bf16).astype(f32)
    for copy in jac_copies:
        copy.wait()

    state_ids = lax.broadcasted_iota(jnp.int32, (state_total, width), 0)

    def to_state(group, total):
        pieces = []
        for k in range(GROUP):
            block = group * GROUP + k
            pieces.append(
                jnp.where(
                    state_ids == jac_state[0, block], merged[pl.ds(block, 1), :], 0.0
                ).astype(bf16)
            )
        rows = pl.ds(pl.multiple_of(group * GROUP * width, GROUP * width), GROUP * width)
        return total + jnp.dot(
            jnp.concatenate(pieces, axis=1), jac[rows, :], preferred_element_type=f32
        )

    blank = jnp.zeros((state_total, width), f32)
    state[...] = (
        lax.fori_loop(0, jac_total // GROUP, to_state, blank, unroll=4).astype(bf16).astype(f32)
    )
    corr_copy.wait()

    def correlate(group, total):
        for k in range(8):
            block = group * 8 + k
            piece = jnp.where(
                state_ids == corr_row[0, block], state[pl.ds(corr_col[0, block], 1), :], 0.0
            ).astype(bf16)
            rows = pl.ds(pl.multiple_of(block * width, width), width)
            total = total + lax.dot_general(
                piece, corr[rows, :], (((1,), (1,)), ((), ())), preferred_element_type=f32
            )
        return total

    spatial = lax.fori_loop(0, corr_total // 8, correlate, blank, unroll=True).astype(bf16)
    spatial_send[...] = spatial

    @pl.when(has_later)
    def _():
        spatial_copy(0, now + 1).start()

    @pl.when(has_earlier)
    def _():
        spatial_copy(1, now - 1).start()

    lax.fori_loop(obs_rows // 2, obs_rows, pick_rows, 0, unroll=2)

    @pl.when(has_earlier)
    def _():
        spatial_copy(0, now - 1).wait_recv()

    @pl.when(now == 0)
    def _():
        spatial_recv[0] = jnp.zeros((state_total, width), bf16)

    @pl.when(has_later)
    def _():
        coupling_copy().wait_recv()
        spatial_copy(1, now + 1).wait_recv()

    @pl.when(now == windows - 1)
    def _():
        spatial_recv[1] = jnp.zeros((state_total, width), bf16)
        coupling_recv[...] = jnp.zeros((state_total, width), bf16)

    coupled[...] = (
        (
            spatial.astype(f32)
            + coupling_ref[...].astype(f32) * spatial_recv[0].astype(f32)
            + coupling_recv[...].astype(f32) * spatial_recv[1].astype(f32)
        )
        .astype(bf16)
        .astype(f32)
    )

    def fetch(group, carry):
        for k in range(GROUP):
            block = group * GROUP + k
            local[pl.ds(block, 1), :] = coupled[pl.ds(jac_state[0, block], 1), :]
        return carry

    lax.fori_loop(0, jac_total // GROUP, fetch, 0, unroll=True)

    group_ids = lax.broadcasted_iota(jnp.int32, (GROUP, width), 0)

    def images(group, carry):
        first = pl.multiple_of(group * GROUP, GROUP)
        rows = pl.ds(pl.multiple_of(group * GROUP * width, GROUP * width), GROUP * width)
        every = lax.dot_general(
            local[pl.ds(first, GROUP), :].astype(bf16),
            jac[rows, :],
            (((1,), (1,)), ((), ())),
            preferred_element_type=f32,
        )
        own = every[:, :width]
        for k in range(1, GROUP):
            own = jnp.where(group_ids == k, every[:, k * width : (k + 1) * width], own)
        portion[pl.ds(pl.multiple_of(me * jac_total + group * GROUP, GROUP), GROUP), :] = (
            own.astype(bf16)
        )
        return carry

    image_part = jac_total // CHUNKS
    groups = image_part // GROUP

    def image_copy(part, step):
        rows = pl.ds(pl.multiple_of(me * jac_total + part * image_part, image_part), image_part)
        return pltpu.make_async_remote_copy(
            src_ref=portion.at[rows],
            dst_ref=portion.at[rows],
            send_sem=image_send.at[part, step - 1],
            recv_sem=image_recv.at[part, step - 1],
            device_id={"tile": peers[step]},
            device_id_type=MESH,
        )

    for part in range(CHUNKS):
        lax.fori_loop(part * groups, (part + 1) * groups, images, 0, unroll=True)
        for step in range(1, tiles):
            image_copy(part, step).start()
    for part in range(CHUNKS):
        for step in range(1, tiles):
            image_copy(part, step).wait_recv()

    out_rows = obs_rows * width // CHUNKS
    out_copies = []
    for part in range(CHUNKS):
        rows = pl.ds(part * out_rows, out_rows)
        gathered = jnp.dot(picker[rows, :], portion[...], preferred_element_type=f32)
        out_ref[rows, :] = (gathered * keeping[rows, :].astype(f32)).astype(bf16)
        copy = pltpu.make_async_copy(out_ref.at[rows], out_hbm.at[rows], out_sem.at[part])
        copy.start()
        out_copies.append(copy)
    for copy in out_copies:
        copy.wait()

    for step, copy in sum_copies:
        copy.wait_send()
    for part in range(CHUNKS):
        for step in range(1, tiles):
            image_copy(part, step).wait_send()

    @pl.when(has_later)
    def _():
        spatial_copy(0, now + 1).wait_send()

    @pl.when(has_earlier)
    def _():
        spatial_copy(1, now - 1).wait_send()
        coupling_copy().wait_send()


def hand_over(held, out, stage, in_sem, out_sem):
    part = held.shape[0] // CHUNKS
    incoming, outgoing = [], []
    for k in range(CHUNKS):
        rows = pl.ds(k * part, part)
        incoming.append(pltpu.make_async_copy(held.at[rows], stage.at[rows], in_sem.at[k]))
        outgoing.append(pltpu.make_async_copy(stage.at[rows], out.at[rows], out_sem.at[k]))
        incoming[-1].start()
    for k in range(CHUNKS):
        incoming[k].wait()
        outgoing[k].start()
    for copy in outgoing:
        copy.wait()


def shards(
    tiles,
    windows,
    obs_values,
    obs_weight,
    obs_count,
    dest_tile,
    jac_index,
    jacobian,
    jac_state,
    corr_blocks,
    corr_row,
    corr_col,
    time_coupling,
):
    f32, bf16 = jnp.float32, jnp.bfloat16
    _, obs_total, width = obs_values.shape
    jac_total = jacobian.shape[1]
    corr_total = corr_blocks.shape[1]
    state_total = time_coupling.shape[1]
    vmem = pl.BlockSpec(memory_space=pltpu.VMEM)
    smem = pl.BlockSpec(memory_space=pltpu.SMEM)
    hbm = pl.BlockSpec(memory_space=pl.ANY)
    dma = pltpu.SemaphoreType.DMA
    out = pl.pallas_call(
        functools.partial(kernel, tiles, windows),
        out_shape=jax.ShapeDtypeStruct((obs_total, width), bf16),
        in_specs=[vmem] * 3 + [hbm] * 3 + [smem, hbm, smem, smem, vmem],
        out_specs=hbm,
        scratch_shapes=[
            pltpu.VMEM((obs_total, width), bf16),
            pltpu.VMEM((obs_total, width), bf16),
            pltpu.VMEM((2, jac_total, obs_total), bf16),
            pltpu.VMEM((obs_total, width), bf16),
            pltpu.VMEM((jac_total * width, width), bf16),
            pltpu.VMEM((corr_total * width, width), bf16),
            pltpu.VMEM((obs_total, tiles * jac_total), bf16),
            pltpu.VMEM((obs_total, width), bf16),
            pltpu.VMEM((obs_total, width), bf16),
            pltpu.VMEM((tiles - 1, jac_total, width), bf16),
            pltpu.VMEM((tiles - 1, jac_total, width), bf16),
            pltpu.VMEM((tiles * jac_total, width), bf16),
            pltpu.VMEM((jac_total, width), f32),
            pltpu.VMEM((state_total, width), f32),
            pltpu.VMEM((state_total, width), f32),
            pltpu.VMEM((jac_total, width), f32),
            pltpu.VMEM((corr_total, width), f32),
            pltpu.VMEM((state_total, width), bf16),
            pltpu.VMEM((2, state_total, width), bf16),
            pltpu.VMEM((state_total, width), bf16),
            dma((2,)),
            dma((CHUNKS,)),
            dma((CHUNKS,)),
            dma,
            dma((tiles - 1,)),
            dma((tiles - 1,)),
            dma((3,)),
            dma((3,)),
            dma((CHUNKS, tiles - 1)),
            dma((CHUNKS, tiles - 1)),
        ],
        compiler_params=pltpu.CompilerParams(
            collective_id=0, has_side_effects=True, vmem_limit_bytes=56 * 1024 * 1024
        ),
        name="dual_space",
    )(
        obs_count.reshape(obs_total // width, width),
        dest_tile.reshape(obs_total // width, width),
        jac_index.reshape(obs_total // width, width),
        obs_values[0],
        obs_weight[0],
        jacobian.reshape(jac_total * width, width),
        jac_state,
        corr_blocks.reshape(corr_total * width, width),
        corr_row,
        corr_col,
        time_coupling[0],
    )
    out = pl.pallas_call(
        hand_over,
        out_shape=jax.ShapeDtypeStruct((obs_total, width), bf16),
        in_specs=[hbm],
        out_specs=hbm,
        scratch_shapes=[
            pltpu.VMEM((obs_total, width), bf16),
            dma((CHUNKS,)),
            dma((CHUNKS,)),
        ],
        name="hand_over",
    )(out)
    return out[None]


def solution(mesh):
    in_specs = (
        P("tm", "tile", None),
        P("tm", "tile", None),
        P("tm", "tile"),
        P("tm", "tile", None),
        P("tm", "tile"),
        P("tm", "tile", None, None),
        P("tm", "tile"),
        P("tm", "tile", None, None),
        P("tm", "tile"),
        P("tm", "tile"),
        P("tm", "tile", None),
    )
    out_specs = P("tm", "tile", None)
    body = functools.partial(shards, mesh.shape["tile"], mesh.shape["tm"])
    return jax.shard_map(body, mesh=mesh, in_specs=in_specs, out_specs=out_specs, check_vma=False)
```

```python
import functools

import jax
import jax.numpy as jnp
from jax import lax
from jax.experimental import pallas as pl
from jax.experimental.pallas import tpu as pltpu
from jax.sharding import PartitionSpec as P

MESH = pl.DeviceIdType.MESH
GROUP = 16
CHUNKS = 4
PARTS = 8


def kernel(
    tiles,
    windows,
    count_ref,
    target_ref,
    column_ref,
    values_hbm,
    weight_hbm,
    jac_hbm,
    jac_state,
    corr_hbm,
    corr_row,
    corr_col,
    coupling_ref,
    portion,
    picker_hbm,
    values_ref,
    weight_ref,
    picks,
    jac,
    corr,
    picker,
    weighted,
    partial,
    arrived,
    image,
    merged,
    state,
    coupled,
    local,
    source,
    spatial_send,
    spatial_recv,
    coupling_recv,
    obs_sem,
    picker_sem,
    own_sem,
    jac_sem,
    corr_sem,
    sum_send,
    sum_recv,
    time_send,
    time_recv,
    image_send,
    image_recv,
):
    f32, bf16 = jnp.float32, jnp.bfloat16
    me = lax.axis_index("tile")
    now = lax.axis_index("tm")
    width = values_ref.shape[1]
    obs_rows = count_ref.shape[0]
    jac_total = merged.shape[0]
    state_total = state.shape[0]
    corr_total = corr_row.shape[1]
    has_earlier, has_later = now > 0, now < windows - 1
    peers = [lax.rem(me + step, tiles) for step in range(tiles)]

    obs_copies = [
        pltpu.make_async_copy(values_hbm, values_ref, obs_sem.at[0]),
        pltpu.make_async_copy(weight_hbm, weight_ref, obs_sem.at[1]),
    ]
    for copy in obs_copies:
        copy.start()
    barrier = pltpu.get_barrier_semaphore()
    for peer in peers[1:]:
        pl.semaphore_signal(barrier, inc=1, device_id={"tile": peer}, device_id_type=MESH)

    @pl.when(has_earlier)
    def _():
        pl.semaphore_signal(barrier, inc=1, device_id={"tm": now - 1}, device_id_type=MESH)

    @pl.when(has_later)
    def _():
        pl.semaphore_signal(barrier, inc=1, device_id={"tm": now + 1}, device_id_type=MESH)

    jac_part = jac.shape[0] // CHUNKS
    jac_copies = []
    for part in range(CHUNKS):
        rows = pl.ds(part * jac_part, jac_part)
        jac_copies.append(pltpu.make_async_copy(jac_hbm.at[rows], jac.at[rows], jac_sem.at[part]))
        jac_copies[-1].start()
    corr_copy = pltpu.make_async_copy(corr_hbm, corr, corr_sem)
    corr_copy.start()

    lane = lax.broadcasted_iota(jnp.int32, (width, width), 1)
    eye = lax.broadcasted_iota(jnp.int32, (width, width), 0) == lane
    ones = jnp.ones((width, width), bf16)

    def upright(ref, row):
        spread = jnp.where(eye, ref[pl.ds(row, 1), :].astype(f32), 0.0).astype(bf16)
        return jnp.dot(spread, ones, preferred_element_type=f32)

    def weigh(row, carry):
        rows = pl.ds(pl.multiple_of(row * width, width), width)
        keep = (lane.astype(f32) < upright(count_ref, row)).astype(f32)
        weighted[rows, :] = (
            values_ref[rows, :].astype(f32) * weight_ref[rows, :].astype(f32) * keep
        ).astype(bf16)
        return carry


    bins = lax.broadcasted_iota(jnp.int32, (jac_total, width), 0)

    def pick_tile(tile, slot):
        def one(row, carry):
            wanted = jnp.where(
                target_ref[pl.ds(row, 1), :] == tile, column_ref[pl.ds(row, 1), :], -1
            )
            columns = pl.ds(pl.multiple_of(row * width, width), width)
            picks[slot, :, columns] = jnp.where(bins == wanted, 1.0, 0.0).astype(bf16)
            return carry

        lax.fori_loop(0, obs_rows, one, 0, unroll=True)

    def partial_sum(slot):
        return jnp.dot(picks[slot], weighted[...], preferred_element_type=f32)

    turns = sorted(range(1, tiles), key=lambda step: -abs(step - tiles // 2)) + [0]
    pick_tile(peers[turns[0]], 0)
    for copy in obs_copies:
        copy.wait()
    lax.fori_loop(0, obs_rows, weigh, 0, unroll=True)

    pl.semaphore_wait(
        barrier,
        tiles - 1 + jnp.where(has_earlier, 1, 0) + jnp.where(has_later, 1, 0),
    )

    def coupling_copy():
        return pltpu.make_async_remote_copy(
            src_ref=coupling_ref,
            dst_ref=coupling_recv,
            send_sem=time_send.at[2],
            recv_sem=time_recv.at[2],
            device_id={"tm": now - 1},
            device_id_type=MESH,
        )

    def spatial_copy(slot, to):
        return pltpu.make_async_remote_copy(
            src_ref=spatial_send,
            dst_ref=spatial_recv.at[slot],
            send_sem=time_send.at[slot],
            recv_sem=time_recv.at[slot],
            device_id={"tm": to},
            device_id_type=MESH,
        )

    @pl.when(has_earlier)
    def _():
        coupling_copy().start()

    sum_copies = []
    for turn, step in enumerate(turns):
        if turn > 0:
            pick_tile(peers[step], turn % 2)
        if step == 0:
            merged[...] = partial_sum(turn % 2)
            continue
        partial[step - 1] = partial_sum(turn % 2).astype(bf16)
        copy = pltpu.make_async_remote_copy(
            src_ref=partial.at[step - 1],
            dst_ref=arrived.at[step - 1],
            send_sem=sum_send.at[step - 1],
            recv_sem=sum_recv.at[step - 1],
            device_id={"tile": peers[step]},
            device_id_type=MESH,
        )
        copy.start()
        sum_copies.append((step, copy))

    lane_f = lane.astype(f32)

    def pick_rows(row, carry):
        rows = pl.ds(pl.multiple_of(row * width, width), width)
        column = upright(column_ref, row)
        target = upright(target_ref, row)
        for tile in range(tiles):
            wanted = jnp.where(target == float(tile), column, -1.0)
            for part in range(jac_total // width):
                start = tile * jac_total + part * width
                picker[rows, start : start + width] = jnp.where(
                    wanted == lane_f + float(part * width), 1.0, 0.0
                ).astype(bf16)
        return carry

    half = obs_rows // 2 * width

    def picker_copy(part):
        rows = pl.ds(part * half, half)
        return pltpu.make_async_copy(picker.at[rows], picker_hbm.at[rows], picker_sem.at[part])

    lax.fori_loop(0, obs_rows // 2, pick_rows, 0, unroll=2)
    picker_copy(0).start()

    for step, copy in sum_copies:
        copy.wait_recv()
        merged[...] += arrived[step - 1].astype(f32)
    merged[...] = merged[...].astype(bf16).astype(f32)
    for copy in jac_copies:
        copy.wait()

    state_ids = lax.broadcasted_iota(jnp.int32, (state_total, width), 0)

    def to_state(group, total):
        pieces = []
        for k in range(GROUP):
            block = group * GROUP + k
            pieces.append(
                jnp.where(
                    state_ids == jac_state[0, block], merged[pl.ds(block, 1), :], 0.0
                ).astype(bf16)
            )
        rows = pl.ds(pl.multiple_of(group * GROUP * width, GROUP * width), GROUP * width)
        return total + jnp.dot(
            jnp.concatenate(pieces, axis=1), jac[rows, :], preferred_element_type=f32
        )

    blank = jnp.zeros((state_total, width), f32)
    state[...] = (
        lax.fori_loop(0, jac_total // GROUP, to_state, blank, unroll=4).astype(bf16).astype(f32)
    )
    corr_copy.wait()

    def correlate(group, total):
        for k in range(8):
            block = group * 8 + k
            piece = jnp.where(
                state_ids == corr_row[0, block], state[pl.ds(corr_col[0, block], 1), :], 0.0
            ).astype(bf16)
            rows = pl.ds(pl.multiple_of(block * width, width), width)
            total = total + lax.dot_general(
                piece, corr[rows, :], (((1,), (1,)), ((), ())), preferred_element_type=f32
            )
        return total

    spatial = lax.fori_loop(0, corr_total // 8, correlate, blank, unroll=True).astype(bf16)
    spatial_send[...] = spatial

    @pl.when(has_later)
    def _():
        spatial_copy(0, now + 1).start()

    @pl.when(has_earlier)
    def _():
        spatial_copy(1, now - 1).start()

    lax.fori_loop(obs_rows // 2, obs_rows, pick_rows, 0, unroll=2)
    picker_copy(1).start()

    @pl.when(has_earlier)
    def _():
        spatial_copy(0, now - 1).wait_recv()

    @pl.when(now == 0)
    def _():
        spatial_recv[0] = jnp.zeros((state_total, width), bf16)

    @pl.when(has_later)
    def _():
        coupling_copy().wait_recv()
        spatial_copy(1, now + 1).wait_recv()

    @pl.when(now == windows - 1)
    def _():
        spatial_recv[1] = jnp.zeros((state_total, width), bf16)
        coupling_recv[...] = jnp.zeros((state_total, width), bf16)

    coupled[...] = (
        (
            spatial.astype(f32)
            + coupling_ref[...].astype(f32) * spatial_recv[0].astype(f32)
            + coupling_recv[...].astype(f32) * spatial_recv[1].astype(f32)
        )
        .astype(bf16)
        .astype(f32)
    )

    def fetch(group, carry):
        for k in range(GROUP):
            block = group * GROUP + k
            local[pl.ds(block, 1), :] = coupled[pl.ds(jac_state[0, block], 1), :]
        return carry

    lax.fori_loop(0, jac_total // GROUP, fetch, 0, unroll=True)

    group_ids = lax.broadcasted_iota(jnp.int32, (GROUP, width), 0)

    def images(group, carry):
        first = pl.multiple_of(group * GROUP, GROUP)
        rows = pl.ds(pl.multiple_of(group * GROUP * width, GROUP * width), GROUP * width)
        every = lax.dot_general(
            local[pl.ds(first, GROUP), :].astype(bf16),
            jac[rows, :],
            (((1,), (1,)), ((), ())),
            preferred_element_type=f32,
        )
        own = every[:, :width]
        for k in range(1, GROUP):
            own = jnp.where(group_ids == k, every[:, k * width : (k + 1) * width], own)
        image[pl.ds(first, GROUP), :] = own.astype(bf16)
        return carry

    image_part = jac_total // CHUNKS
    groups = image_part // GROUP

    def image_copy(part, step):
        rows = pl.ds(pl.multiple_of(me * jac_total + part * image_part, image_part), image_part)
        return pltpu.make_async_remote_copy(
            src_ref=image.at[pl.ds(part * image_part, image_part)],
            dst_ref=portion.at[rows],
            send_sem=image_send.at[part, step - 1],
            recv_sem=image_recv.at[part, step - 1],
            device_id={"tile": peers[step]},
            device_id_type=MESH,
        )

    for part in range(CHUNKS):
        lax.fori_loop(part * groups, (part + 1) * groups, images, 0, unroll=True)
        for step in range(1, tiles):
            image_copy(part, step).start()
    own_copy = pltpu.make_async_copy(
        image, portion.at[pl.ds(pl.multiple_of(me * jac_total, jac_total), jac_total)], own_sem
    )
    own_copy.start()
    for part in range(CHUNKS):
        for step in range(1, tiles):
            image_copy(part, step).wait_recv()
    own_copy.wait()

    picker_copy(0).wait()
    picker_copy(1).wait()
    for step, copy in sum_copies:
        copy.wait_send()
    for part in range(CHUNKS):
        for step in range(1, tiles):
            image_copy(part, step).wait_send()

    @pl.when(has_later)
    def _():
        spatial_copy(0, now + 1).wait_send()

    @pl.when(has_earlier)
    def _():
        spatial_copy(1, now - 1).wait_send()
        coupling_copy().wait_send()


def gather(
    count_ref,
    portion_hbm,
    picker_hbm,
    out_hbm,
    portion,
    picker,
    keeping,
    out_ref,
    portion_sem,
    in_sem,
    out_sem,
):
    f32, bf16 = jnp.float32, jnp.bfloat16
    width = out_ref.shape[1]
    part = out_ref.shape[0] // PARTS
    portion_copy = pltpu.make_async_copy(portion_hbm, portion, portion_sem)
    portion_copy.start()
    incoming, outgoing = [], []
    for k in range(PARTS):
        rows = pl.ds(k * part, part)
        incoming.append(pltpu.make_async_copy(picker_hbm.at[rows], picker.at[rows], in_sem.at[k]))
        outgoing.append(pltpu.make_async_copy(out_ref.at[rows], out_hbm.at[rows], out_sem.at[k]))
        incoming[-1].start()
    lane = lax.broadcasted_iota(jnp.int32, (width, width), 1)
    eye = lax.broadcasted_iota(jnp.int32, (width, width), 0) == lane
    ones = jnp.ones((width, width), bf16)
    for row in range(count_ref.shape[0]):
        spread = jnp.where(eye, count_ref[row : row + 1, :].astype(f32), 0.0).astype(bf16)
        count = jnp.dot(spread, ones, preferred_element_type=f32)
        keeping[row * width : (row + 1) * width, :] = (lane.astype(f32) < count).astype(f32)
    portion_copy.wait()
    for k in range(PARTS):
        rows = pl.ds(k * part, part)
        incoming[k].wait()
        gathered = jnp.dot(picker[rows, :], portion[...], preferred_element_type=f32)
        out_ref[rows, :] = (gathered * keeping[rows, :]).astype(bf16)
        outgoing[k].start()
    for copy in outgoing:
        copy.wait()


def shards(
    tiles,
    windows,
    obs_values,
    obs_weight,
    obs_count,
    dest_tile,
    jac_index,
    jacobian,
    jac_state,
    corr_blocks,
    corr_row,
    corr_col,
    time_coupling,
):
    f32, bf16 = jnp.float32, jnp.bfloat16
    _, obs_total, width = obs_values.shape
    jac_total = jacobian.shape[1]
    corr_total = corr_blocks.shape[1]
    state_total = time_coupling.shape[1]
    vmem = pl.BlockSpec(memory_space=pltpu.VMEM)
    smem = pl.BlockSpec(memory_space=pltpu.SMEM)
    hbm = pl.BlockSpec(memory_space=pl.ANY)
    dma = pltpu.SemaphoreType.DMA
    portion, picker = pl.pallas_call(
        functools.partial(kernel, tiles, windows),
        out_shape=(
            jax.ShapeDtypeStruct((tiles * jac_total, width), bf16),
            jax.ShapeDtypeStruct((obs_total, tiles * jac_total), bf16),
        ),
        in_specs=[vmem] * 3 + [hbm] * 3 + [smem, hbm, smem, smem, vmem],
        out_specs=(hbm, hbm),
        scratch_shapes=[
            pltpu.VMEM((obs_total, width), bf16),
            pltpu.VMEM((obs_total, width), bf16),
            pltpu.VMEM((2, jac_total, obs_total), bf16),
            pltpu.VMEM((jac_total * width, width), bf16),
            pltpu.VMEM((corr_total * width, width), bf16),
            pltpu.VMEM((obs_total, tiles * jac_total), bf16),
            pltpu.VMEM((obs_total, width), bf16),
            pltpu.VMEM((tiles - 1, jac_total, width), bf16),
            pltpu.VMEM((tiles - 1, jac_total, width), bf16),
            pltpu.VMEM((jac_total, width), bf16),
            pltpu.VMEM((jac_total, width), f32),
            pltpu.VMEM((state_total, width), f32),
            pltpu.VMEM((state_total, width), f32),
            pltpu.VMEM((jac_total, width), f32),
            pltpu.VMEM((corr_total, width), f32),
            pltpu.VMEM((state_total, width), bf16),
            pltpu.VMEM((2, state_total, width), bf16),
            pltpu.VMEM((state_total, width), bf16),
            dma((2,)),
            dma((2,)),
            dma,
            dma((CHUNKS,)),
            dma,
            dma((tiles - 1,)),
            dma((tiles - 1,)),
            dma((3,)),
            dma((3,)),
            dma((CHUNKS, tiles - 1)),
            dma((CHUNKS, tiles - 1)),
        ],
        compiler_params=pltpu.CompilerParams(
            collective_id=0, has_side_effects=True, vmem_limit_bytes=56 * 1024 * 1024
        ),
        name="dual_space",
    )(
        obs_count.reshape(obs_total // width, width),
        dest_tile.reshape(obs_total // width, width),
        jac_index.reshape(obs_total // width, width),
        obs_values[0],
        obs_weight[0],
        jacobian.reshape(jac_total * width, width),
        jac_state,
        corr_blocks.reshape(corr_total * width, width),
        corr_row,
        corr_col,
        time_coupling[0],
    )
    out = pl.pallas_call(
        gather,
        out_shape=jax.ShapeDtypeStruct((obs_total, width), bf16),
        in_specs=[vmem, hbm, hbm],
        out_specs=hbm,
        scratch_shapes=[
            pltpu.VMEM((tiles * jac_total, width), bf16),
            pltpu.VMEM((obs_total, tiles * jac_total), bf16),
            pltpu.VMEM((obs_total, width), f32),
            pltpu.VMEM((obs_total, width), bf16),
            dma,
            dma((PARTS,)),
            dma((PARTS,)),
        ],
        compiler_params=pltpu.CompilerParams(vmem_limit_bytes=56 * 1024 * 1024),
        name="gather",
    )(obs_count.reshape(obs_total // width, width), portion, picker)
    return out[None]


def solution(mesh):
    in_specs = (
        P("tm", "tile", None),
        P("tm", "tile", None),
        P("tm", "tile"),
        P("tm", "tile", None),
        P("tm", "tile"),
        P("tm", "tile", None, None),
        P("tm", "tile"),
        P("tm", "tile", None, None),
        P("tm", "tile"),
        P("tm", "tile"),
        P("tm", "tile", None),
    )
    out_specs = P("tm", "tile", None)
    body = functools.partial(shards, mesh.shape["tile"], mesh.shape["tm"])
    return jax.shard_map(body, mesh=mesh, in_specs=in_specs, out_specs=out_specs, check_vma=False)
```

```python
import functools

import jax
import jax.numpy as jnp
from jax import lax
from jax.experimental import pallas as pl
from jax.experimental.pallas import tpu as pltpu
from jax.sharding import PartitionSpec as P

MESH = pl.DeviceIdType.MESH
GROUP = 16
CHUNKS = 4


def kernel(
    tiles,
    windows,
    count_ref,
    target_ref,
    column_ref,
    values_hbm,
    weight_hbm,
    jac_hbm,
    jac_state,
    corr_hbm,
    corr_row,
    corr_col,
    coupling_ref,
    out_hbm,
    values_ref,
    weight_ref,
    picks,
    early,
    out_ref,
    jac,
    corr,
    picker,
    weighted,
    keeping,
    partial,
    arrived,
    portion,
    merged,
    state,
    coupled,
    local,
    source,
    spatial_send,
    spatial_recv,
    coupling_recv,
    obs_sem,
    out_sem,
    jac_sem,
    corr_sem,
    sum_send,
    sum_recv,
    time_send,
    time_recv,
    image_send,
    image_recv,
):
    f32, bf16 = jnp.float32, jnp.bfloat16
    me = lax.axis_index("tile")
    now = lax.axis_index("tm")
    width = values_ref.shape[1]
    obs_rows = count_ref.shape[0]
    jac_total = merged.shape[0]
    state_total = state.shape[0]
    corr_total = corr_row.shape[1]
    has_earlier, has_later = now > 0, now < windows - 1
    peers = [lax.rem(me + step, tiles) for step in range(tiles)]

    obs_copies = [
        pltpu.make_async_copy(values_hbm, values_ref, obs_sem.at[0]),
        pltpu.make_async_copy(weight_hbm, weight_ref, obs_sem.at[1]),
    ]
    for copy in obs_copies:
        copy.start()
    barrier = pltpu.get_barrier_semaphore()
    for peer in peers[1:]:
        pl.semaphore_signal(barrier, inc=1, device_id={"tile": peer}, device_id_type=MESH)

    @pl.when(has_earlier)
    def _():
        pl.semaphore_signal(barrier, inc=1, device_id={"tm": now - 1}, device_id_type=MESH)

    @pl.when(has_later)
    def _():
        pl.semaphore_signal(barrier, inc=1, device_id={"tm": now + 1}, device_id_type=MESH)

    jac_part = jac.shape[0] // CHUNKS
    jac_copies = []
    for part in range(CHUNKS):
        rows = pl.ds(part * jac_part, jac_part)
        jac_copies.append(pltpu.make_async_copy(jac_hbm.at[rows], jac.at[rows], jac_sem.at[part]))
        jac_copies[-1].start()
    corr_copy = pltpu.make_async_copy(corr_hbm, corr, corr_sem)
    corr_copy.start()

    lane = lax.broadcasted_iota(jnp.int32, (width, width), 1)
    eye = lax.broadcasted_iota(jnp.int32, (width, width), 0) == lane
    ones = jnp.ones((width, width), bf16)

    def upright(ref, row):
        spread = jnp.where(eye, ref[pl.ds(row, 1), :].astype(f32), 0.0).astype(bf16)
        return jnp.dot(spread, ones, preferred_element_type=f32)

    def weigh(row, carry):
        rows = pl.ds(pl.multiple_of(row * width, width), width)
        keep = (lane.astype(f32) < upright(count_ref, row)).astype(f32)
        keeping[rows, :] = keep.astype(bf16)
        weighted[rows, :] = (
            values_ref[rows, :].astype(f32) * weight_ref[rows, :].astype(f32) * keep
        ).astype(bf16)
        return carry


    bins = lax.broadcasted_iota(jnp.int32, (jac_total, width), 0)

    def pick_tile(tile, slot):
        def one(row, carry):
            wanted = jnp.where(
                target_ref[pl.ds(row, 1), :] == tile, column_ref[pl.ds(row, 1), :], -1
            )
            columns = pl.ds(pl.multiple_of(row * width, width), width)
            picks[slot, :, columns] = jnp.where(bins == wanted, 1.0, 0.0).astype(bf16)
            return carry

        lax.fori_loop(0, obs_rows, one, 0, unroll=True)

    def partial_sum(slot):
        return jnp.dot(picks[slot], weighted[...], preferred_element_type=f32)

    turns = sorted(range(1, tiles), key=lambda step: -abs(step - tiles // 2)) + [0]
    pick_tile(peers[turns[0]], 0)
    for copy in obs_copies:
        copy.wait()
    lax.fori_loop(0, obs_rows, weigh, 0, unroll=True)

    pl.semaphore_wait(
        barrier,
        tiles - 1 + jnp.where(has_earlier, 1, 0) + jnp.where(has_later, 1, 0),
    )

    def coupling_copy():
        return pltpu.make_async_remote_copy(
            src_ref=coupling_ref,
            dst_ref=coupling_recv,
            send_sem=time_send.at[2],
            recv_sem=time_recv.at[2],
            device_id={"tm": now - 1},
            device_id_type=MESH,
        )

    def spatial_copy(slot, to):
        return pltpu.make_async_remote_copy(
            src_ref=spatial_send,
            dst_ref=spatial_recv.at[slot],
            send_sem=time_send.at[slot],
            recv_sem=time_recv.at[slot],
            device_id={"tm": to},
            device_id_type=MESH,
        )

    @pl.when(has_earlier)
    def _():
        coupling_copy().start()

    sum_copies = []
    for turn, step in enumerate(turns):
        if turn > 0:
            pick_tile(peers[step], turn % 2)
        if step == 0:
            merged[...] = partial_sum(turn % 2)
            continue
        partial[step - 1] = partial_sum(turn % 2).astype(bf16)
        copy = pltpu.make_async_remote_copy(
            src_ref=partial.at[step - 1],
            dst_ref=arrived.at[step - 1],
            send_sem=sum_send.at[step - 1],
            recv_sem=sum_recv.at[step - 1],
            device_id={"tile": peers[step]},
            device_id_type=MESH,
        )
        copy.start()
        sum_copies.append((step, copy))

    lane_f = lane.astype(f32)
    image_part = jac_total // CHUNKS

    def pick_rows(row, carry):
        rows = pl.ds(pl.multiple_of(row * width, width), width)
        column = upright(column_ref, row)
        target = upright(target_ref, row)
        part = jnp.floor(column * (1.0 / image_part))
        wanted = column + float(image_part) * (target + float(tiles - 1) * part)
        for start in range(0, tiles * jac_total, width):
            picker[rows, start : start + width] = jnp.where(
                wanted == lane_f + float(start), 1.0, 0.0
            ).astype(bf16)
        return carry

    lax.fori_loop(0, obs_rows // 2, pick_rows, 0, unroll=2)

    for step, copy in sum_copies:
        copy.wait_recv()
        merged[...] += arrived[step - 1].astype(f32)
    merged[...] = merged[...].astype(bf16).astype(f32)

    state_ids = lax.broadcasted_iota(jnp.int32, (state_total, width), 0)

    def to_state(group, total):
        pieces = []
        for k in range(GROUP):
            block = group * GROUP + k
            pieces.append(
                jnp.where(
                    state_ids == jac_state[0, block], merged[pl.ds(block, 1), :], 0.0
                ).astype(bf16)
            )
        rows = pl.ds(pl.multiple_of(group * GROUP * width, GROUP * width), GROUP * width)
        return total + jnp.dot(
            jnp.concatenate(pieces, axis=1), jac[rows, :], preferred_element_type=f32
        )

    blank = jnp.zeros((state_total, width), f32)
    quarter = jac_total // GROUP // CHUNKS
    gained = blank
    for part in range(CHUNKS):
        jac_copies[part].wait()
        gained = lax.fori_loop(
            part * quarter, (part + 1) * quarter, to_state, gained, unroll=True
        )
    state[...] = gained.astype(bf16).astype(f32)
    corr_copy.wait()

    def correlate(group, total):
        for k in range(8):
            block = group * 8 + k
            piece = jnp.where(
                state_ids == corr_row[0, block], state[pl.ds(corr_col[0, block], 1), :], 0.0
            ).astype(bf16)
            rows = pl.ds(pl.multiple_of(block * width, width), width)
            total = total + lax.dot_general(
                piece, corr[rows, :], (((1,), (1,)), ((), ())), preferred_element_type=f32
            )
        return total

    spatial = lax.fori_loop(0, corr_total // 8, correlate, blank, unroll=True).astype(bf16)
    spatial_send[...] = spatial

    @pl.when(has_later)
    def _():
        spatial_copy(0, now + 1).start()

    @pl.when(has_earlier)
    def _():
        spatial_copy(1, now - 1).start()

    lax.fori_loop(obs_rows // 2, obs_rows, pick_rows, 0, unroll=2)

    @pl.when(has_earlier)
    def _():
        spatial_copy(0, now - 1).wait_recv()

    @pl.when(now == 0)
    def _():
        spatial_recv[0] = jnp.zeros((state_total, width), bf16)

    @pl.when(has_later)
    def _():
        coupling_copy().wait_recv()
        spatial_copy(1, now + 1).wait_recv()

    @pl.when(now == windows - 1)
    def _():
        spatial_recv[1] = jnp.zeros((state_total, width), bf16)
        coupling_recv[...] = jnp.zeros((state_total, width), bf16)

    coupled[...] = (
        (
            spatial.astype(f32)
            + coupling_ref[...].astype(f32) * spatial_recv[0].astype(f32)
            + coupling_recv[...].astype(f32) * spatial_recv[1].astype(f32)
        )
        .astype(bf16)
        .astype(f32)
    )

    def fetch(group, carry):
        for k in range(GROUP):
            block = group * GROUP + k
            local[pl.ds(block, 1), :] = coupled[pl.ds(jac_state[0, block], 1), :]
        return carry

    lax.fori_loop(0, jac_total // GROUP, fetch, 0, unroll=True)

    group_ids = lax.broadcasted_iota(jnp.int32, (GROUP, width), 0)

    def images(group, carry):
        first = pl.multiple_of(group * GROUP, GROUP)
        rows = pl.ds(pl.multiple_of(group * GROUP * width, GROUP * width), GROUP * width)
        every = lax.dot_general(
            local[pl.ds(first, GROUP), :].astype(bf16),
            jac[rows, :],
            (((1,), (1,)), ((), ())),
            preferred_element_type=f32,
        )
        own = every[:, :width]
        for k in range(1, GROUP):
            own = jnp.where(group_ids == k, every[:, k * width : (k + 1) * width], own)
        part = group // groups
        row = (part * tiles + me) * image_part + (group - part * groups) * GROUP
        portion[pl.ds(pl.multiple_of(row, GROUP), GROUP), :] = own.astype(bf16)
        return carry

    groups = image_part // GROUP

    def image_copy(part, step):
        rows = pl.ds(pl.multiple_of((part * tiles + me) * image_part, image_part), image_part)
        return pltpu.make_async_remote_copy(
            src_ref=portion.at[rows],
            dst_ref=portion.at[rows],
            send_sem=image_send.at[part, step - 1],
            recv_sem=image_recv.at[part, step - 1],
            device_id={"tile": peers[step]},
            device_id_type=MESH,
        )

    for part in range(CHUNKS):
        lax.fori_loop(part * groups, (part + 1) * groups, images, 0, unroll=True)
        for step in range(1, tiles):
            image_copy(part, step).start()
    out_rows = obs_rows * width // CHUNKS
    ready = (CHUNKS - 1) * tiles * image_part
    for part in range(CHUNKS - 1):
        for step in range(1, tiles):
            image_copy(part, step).wait_recv()
    for part in range(CHUNKS):
        rows = pl.ds(part * out_rows, out_rows)
        early[rows, :] = jnp.dot(
            picker[rows, :ready], portion[:ready, :], preferred_element_type=f32
        )
    for step in range(1, tiles):
        image_copy(CHUNKS - 1, step).wait_recv()
    out_copies = []
    for part in range(CHUNKS):
        rows = pl.ds(part * out_rows, out_rows)
        gathered = early[rows, :] + jnp.dot(
            picker[rows, ready:], portion[ready:, :], preferred_element_type=f32
        )
        out_ref[rows, :] = (gathered * keeping[rows, :].astype(f32)).astype(bf16)
        copy = pltpu.make_async_copy(out_ref.at[rows], out_hbm.at[rows], out_sem.at[part])
        copy.start()
        out_copies.append(copy)
    for copy in out_copies:
        copy.wait()

    for step, copy in sum_copies:
        copy.wait_send()
    for part in range(CHUNKS):
        for step in range(1, tiles):
            image_copy(part, step).wait_send()

    @pl.when(has_later)
    def _():
        spatial_copy(0, now + 1).wait_send()

    @pl.when(has_earlier)
    def _():
        spatial_copy(1, now - 1).wait_send()
        coupling_copy().wait_send()


def hand_over(held, out, stage, in_sem, out_sem):
    part = held.shape[0] // CHUNKS
    incoming, outgoing = [], []
    for k in range(CHUNKS):
        rows = pl.ds(k * part, part)
        incoming.append(pltpu.make_async_copy(held.at[rows], stage.at[rows], in_sem.at[k]))
        outgoing.append(pltpu.make_async_copy(stage.at[rows], out.at[rows], out_sem.at[k]))
        incoming[-1].start()
    for k in range(CHUNKS):
        incoming[k].wait()
        outgoing[k].start()
    for copy in outgoing:
        copy.wait()


def shards(
    tiles,
    windows,
    obs_values,
    obs_weight,
    obs_count,
    dest_tile,
    jac_index,
    jacobian,
    jac_state,
    corr_blocks,
    corr_row,
    corr_col,
    time_coupling,
):
    f32, bf16 = jnp.float32, jnp.bfloat16
    _, obs_total, width = obs_values.shape
    jac_total = jacobian.shape[1]
    corr_total = corr_blocks.shape[1]
    state_total = time_coupling.shape[1]
    vmem = pl.BlockSpec(memory_space=pltpu.VMEM)
    smem = pl.BlockSpec(memory_space=pltpu.SMEM)
    hbm = pl.BlockSpec(memory_space=pl.ANY)
    dma = pltpu.SemaphoreType.DMA
    out = pl.pallas_call(
        functools.partial(kernel, tiles, windows),
        out_shape=jax.ShapeDtypeStruct((obs_total, width), bf16),
        in_specs=[vmem] * 3 + [hbm] * 3 + [smem, hbm, smem, smem, vmem],
        out_specs=hbm,
        scratch_shapes=[
            pltpu.VMEM((obs_total, width), bf16),
            pltpu.VMEM((obs_total, width), bf16),
            pltpu.VMEM((2, jac_total, obs_total), bf16),
            pltpu.VMEM((obs_total, width), f32),
            pltpu.VMEM((obs_total, width), bf16),
            pltpu.VMEM((jac_total * width, width), bf16),
            pltpu.VMEM((corr_total * width, width), bf16),
            pltpu.VMEM((obs_total, tiles * jac_total), bf16),
            pltpu.VMEM((obs_total, width), bf16),
            pltpu.VMEM((obs_total, width), bf16),
            pltpu.VMEM((tiles - 1, jac_total, width), bf16),
            pltpu.VMEM((tiles - 1, jac_total, width), bf16),
            pltpu.VMEM((tiles * jac_total, width), bf16),
            pltpu.VMEM((jac_total, width), f32),
            pltpu.VMEM((state_total, width), f32),
            pltpu.VMEM((state_total, width), f32),
            pltpu.VMEM((jac_total, width), f32),
            pltpu.VMEM((corr_total, width), f32),
            pltpu.VMEM((state_total, width), bf16),
            pltpu.VMEM((2, state_total, width), bf16),
            pltpu.VMEM((state_total, width), bf16),
            dma((2,)),
            dma((CHUNKS,)),
            dma((CHUNKS,)),
            dma,
            dma((tiles - 1,)),
            dma((tiles - 1,)),
            dma((3,)),
            dma((3,)),
            dma((CHUNKS, tiles - 1)),
            dma((CHUNKS, tiles - 1)),
        ],
        compiler_params=pltpu.CompilerParams(
            collective_id=0, has_side_effects=True, vmem_limit_bytes=56 * 1024 * 1024
        ),
        name="dual_space",
    )(
        obs_count.reshape(obs_total // width, width),
        dest_tile.reshape(obs_total // width, width),
        jac_index.reshape(obs_total // width, width),
        obs_values[0],
        obs_weight[0],
        jacobian.reshape(jac_total * width, width),
        jac_state,
        corr_blocks.reshape(corr_total * width, width),
        corr_row,
        corr_col,
        time_coupling[0],
    )
    out = pl.pallas_call(
        hand_over,
        out_shape=jax.ShapeDtypeStruct((obs_total, width), bf16),
        in_specs=[hbm],
        out_specs=hbm,
        scratch_shapes=[
            pltpu.VMEM((obs_total, width), bf16),
            dma((CHUNKS,)),
            dma((CHUNKS,)),
        ],
        name="hand_over",
    )(out)
    return out[None]


def solution(mesh):
    in_specs = (
        P("tm", "tile", None),
        P("tm", "tile", None),
        P("tm", "tile"),
        P("tm", "tile", None),
        P("tm", "tile"),
        P("tm", "tile", None, None),
        P("tm", "tile"),
        P("tm", "tile", None, None),
        P("tm", "tile"),
        P("tm", "tile"),
        P("tm", "tile", None),
    )
    out_specs = P("tm", "tile", None)
    body = functools.partial(shards, mesh.shape["tile"], mesh.shape["tm"])
    return jax.shard_map(body, mesh=mesh, in_specs=in_specs, out_specs=out_specs, check_vma=False)
```
